32 devices in a mesh: gx: 4 (over z), gy: 4 (over x, core), gz: 2 (over y).
Axes of the slice: x: 2, y: 2, z: 4, core: 2. Of those that a mesh axis runs over, the one named last changes fastest.
Arguments:
- tokens: bfloat16 [2048, 6144], P(('gy', 'gx'), 'gz'), may hold values from -6 to 6
- w_in: bfloat16 [6144, 24576], P('gz', ('gx', 'gy')), may hold values from -0.078125 to 0.078125
- w_out: bfloat16 [24576, 6144], P(('gx', 'gy'), 'gz')
- out_grad: bfloat16 [2048, 6144], P(('gy', 'gx'), 'gz')
Outputs:
- in_grad: bfloat16 [2048, 6144], P(('gy', 'gx'), 'gz')
- grad_in_clipped: bfloat16 [6144, 24576], P('gz', ('gx', 'gy'))
- grad_out_clipped: bfloat16 [24576, 6144], P(('gx', 'gy'), 'gz')
The draws below stay inside these ranges and needn't reach their ends.
All inputs are finite; a program needn't handle non-finite values.
Results may differ from the reference program's by a relative error of at most 0.025.
Values may be sent and summed in bfloat16 or wider, within the bound.
No kernel may reach another device: no remote copies, remote signals or barrier semaphores. Data moves between devices by JAX's collectives and lax.ppermute only.
A program may use at most 384 MiB of HBM per device.

```python
import math
import jax
import jax.numpy as jnp
from jax import lax

D = 6144
FW = 24576
TOKENS = 2048
N_GZ = 2


def rising_scales(key, count):
    uniform_part = jax.random.uniform(key, (count,), jnp.float32)
    position = jnp.arange(count, dtype=jnp.float32) / count
    return jnp.exp(math.log(3.0) * position + math.log(10.0 / 3.0) * uniform_part)


def draw_w_out(key, part):
    key = jax.random.fold_in(key, 11)
    key_one, key_two = jax.random.split(key)
    row_scale = rising_scales(key_two, FW)
    base = jnp.clip(jax.random.normal(key_one, (FW, D), jnp.float32), -6.0, 6.0)
    return (base * row_scale[:, None] / (4.0 * math.sqrt(FW))).astype(jnp.bfloat16)


def draw_out_grad(key, part):
    key = jax.random.fold_in(key, 23)
    key_one, key_two, key_three = jax.random.split(key, 3)
    col_scale = rising_scales(key_two, D)
    row_scale = jnp.exp(math.log(10.0) * jax.random.uniform(key_three, (TOKENS,), jnp.float32))
    base = jnp.clip(jax.random.normal(key_one, (TOKENS, D), jnp.float32), -6.0, 6.0)
    return (base * col_scale[None, :] * row_scale[:, None] / 10.0).astype(jnp.bfloat16)


def block_levels(stream_key, shape, pieces, smallest, largest):
    factor_of, own = 1.0, jax.random.fold_in(stream_key, 6)
    for axis_at, blocks in pieces:
        heights = jnp.exp(jax.random.uniform(jax.random.fold_in(own, axis_at), (blocks,), jnp.float32, smallest / len(pieces), largest / len(pieces)))
        factor_of = factor_of * jnp.repeat(heights, shape[axis_at] // blocks).reshape([-1 if axis == axis_at else 1 for axis in range(len(shape))])
    return factor_of


def bell_draw(stream_key, extent, width, reach, cuts=(), held_as=jnp.bfloat16):
    drawn = width * jax.random.normal(stream_key, extent, jnp.float32)
    if cuts:
        drawn = drawn * block_levels(stream_key, extent, cuts, -0.22, 0.18)
    return jnp.clip(drawn, -reach, reach).astype(held_as)


def setup_inputs(seed: int = 0) -> dict:
    key_of = jax.random.split(jax.random.key(seed), 5)
    tokens = bell_draw(key_of[0], (TOKENS, D), 1.0, 6.0, ((0, 16), (1, 2)))
    w_in = bell_draw(key_of[1], (D, FW), D ** -0.5, 0.078125, ((0, 2), (1, 16)))
    w_out = draw_w_out(jax.random.fold_in(key_of[4], 71), 0)
    out_grad = draw_out_grad(jax.random.fold_in(key_of[4], 71), 0)
    return dict(tokens=tokens, w_in=w_in, w_out=w_out, out_grad=out_grad)


GELU_C = 0.7978845608

def gelu_parts(values):
    inner_arg = GELU_C * (values + 0.044715 * values * values * values)
    tanh_val = jnp.tanh(inner_arg)
    value_out = 0.5 * values * (1.0 + tanh_val)
    slope = 0.5 * (1.0 + tanh_val) + 0.5 * values * (1.0 - tanh_val * tanh_val) * GELU_C * (1.0 + 3.0 * 0.044715 * values * values)
    return (value_out, slope)

def reference(tokens, w_in, w_out, out_grad):
    width_blk = D // N_GZ

    def add_block(running, block_id):
        start = (block_id * width_blk).astype(jnp.int32)
        x_part = lax.dynamic_slice_in_dim(tokens, start, width_blk, 1)
        w_part = lax.dynamic_slice_in_dim(w_in, start, width_blk, 0)
        dy_part = lax.dynamic_slice_in_dim(out_grad, start, width_blk, 1)
        o_part = lax.dynamic_slice_in_dim(w_out, start, width_blk, 1)
        h_term = jnp.dot(x_part, w_part, preferred_element_type=jnp.float32)
        d_term = lax.dot_general(dy_part, o_part, (((1,), (1,)), ((), ())), preferred_element_type=jnp.float32)
        h_term = lax.optimization_barrier(h_term.astype(jnp.bfloat16)).astype(jnp.float32)
        d_term = lax.optimization_barrier(d_term.astype(jnp.bfloat16)).astype(jnp.float32)
        return ((running[0] + h_term, running[1] + d_term), None)
    zeros_init = jnp.zeros((TOKENS, FW), jnp.float32)
    (pre_act, d_act), _ = lax.scan(add_block, (zeros_init, zeros_init), jnp.arange(N_GZ, dtype=jnp.int32))
    value_out, slope = gelu_parts(pre_act)
    act_rows = value_out.astype(jnp.bfloat16)
    d_pre = (d_act * slope).astype(jnp.bfloat16)
    in_grad = lax.dot_general(d_pre, w_in, (((1,), (1,)), ((), ())), preferred_element_type=jnp.float32).astype(jnp.bfloat16)
    grad_in = lax.dot_general(tokens, d_pre, (((0,), (0,)), ((), ())), preferred_element_type=jnp.float32)
    grad_out = lax.dot_general(act_rows, out_grad, (((0,), (0,)), ((), ())), preferred_element_type=jnp.float32)
    square_sum = jnp.sum(grad_in * grad_in) + jnp.sum(grad_out * grad_out)
    factor = 1.0 / jnp.sqrt(square_sum / (2.0 * D * FW) + 1e-06)
    return (in_grad, (grad_in * factor).astype(jnp.bfloat16), (grad_out * factor).astype(jnp.bfloat16))
```

```python
import jax
import jax.numpy as jnp
from jax import lax
from jax.experimental import pallas as pl
from jax.experimental.pallas import tpu as pltpu
from jax.sharding import PartitionSpec as P

GELU_C = 0.7978845608
MIB = 1 << 20
ANY = pl.BlockSpec(memory_space=pl.ANY)
HELD = pl.BlockSpec(memory_space=pltpu.VMEM)


def gelu_parts(values):
    inner_arg = GELU_C * (values + 0.044715 * values * values * values)
    tanh_val = jnp.tanh(inner_arg)
    value_out = 0.5 * values * (1.0 + tanh_val)
    slope = 0.5 * (1.0 + tanh_val) + 0.5 * values * (1.0 - tanh_val * tanh_val) * GELU_C * (
        1.0 + 3.0 * 0.044715 * values * values
    )
    return (value_out, slope)


def contract(left, right, left_dim, right_dim):
    return lax.dot_general(
        left, right, (((left_dim,), (right_dim,)), ((), ())), preferred_element_type=jnp.float32
    )


def tile_of(extent, most):
    size = most
    while extent % size:
        size //= 2
    return size


def stacked(refs):
    return jnp.concatenate([ref[...] for ref in refs], axis=0) if len(refs) > 1 else refs[0][...]


def params(mib):
    return pltpu.CompilerParams(vmem_limit_bytes=mib * MIB)


def flip_call(weight, after):
    rows, cols = weight.shape
    tile = tile_of(cols, 256)

    def kernel(in_ref, *refs):
        refs[-1][...] = in_ref[...].T

    return pl.pallas_call(
        kernel,
        grid=(cols // tile,),
        in_specs=[pl.BlockSpec((rows, tile), lambda i: (0, i))] + [ANY] * len(after),
        out_specs=pl.BlockSpec((tile, rows), lambda i: (i, 0)),
        out_shape=jax.ShapeDtypeStruct((cols, rows), weight.dtype),
        compiler_params=params(16),
        name="flip",
    )(weight, *after)


def terms_call(blocks, w_in, w_out, after, held):
    hidden, depth = w_out.shape
    rows = blocks[0].shape[0] // 2
    count = len(blocks)
    tile = tile_of(hidden, 768 if held else 384)
    steps = hidden // tile

    def kernel(*refs):
        x_refs, dy_refs = refs[:count], refs[count : 2 * count]
        w_in_ref, w_out_ref = refs[2 * count : 2 * count + 2]
        out_ref = refs[-1]
        step = pl.program_id(0)

        @pl.when(step < steps)
        def _():
            at = pl.ds(pl.multiple_of(step * tile, tile), tile) if held else slice(None)
            out_ref[...] = contract(w_in_ref[at, :], stacked(x_refs), 1, 1).astype(jnp.bfloat16)

        @pl.when(step >= steps)
        def _():
            at = pl.ds(pl.multiple_of((step - steps) * tile, tile), tile) if held else slice(None)
            out_ref[...] = contract(w_out_ref[at, :], stacked(dy_refs), 1, 1).astype(jnp.bfloat16)

    w_specs = [HELD, HELD]
    if not held:
        w_specs = [
            pl.BlockSpec((tile, depth), lambda i: (jnp.minimum(i, steps - 1), 0)),
            pl.BlockSpec((tile, depth), lambda i: (jnp.maximum(i - steps, 0), 0)),
        ]
    return pl.pallas_call(
        kernel,
        grid=(2 * steps,),
        in_specs=[pl.BlockSpec((rows, depth), lambda i: (0, 0))] * count
        + [pl.BlockSpec((rows, depth), lambda i: (1, 0))] * count
        + w_specs
        + [ANY] * len(after),
        out_specs=pl.BlockSpec((tile, count * rows), lambda i: (i, 0)),
        out_shape=jax.ShapeDtypeStruct((2 * hidden, count * rows), jnp.bfloat16),
        compiler_params=params(12 if held else 24),
        name="terms",
    )(*blocks, *blocks, w_in, w_out, *after)


def half_call(blocks, part, weight, weight_dim, after):
    depth, hidden = weight.shape[weight_dim], weight.shape[1 - weight_dim]
    rows = blocks[0].shape[0] // 2
    count = len(blocks)
    tile = tile_of(hidden, 384)

    def kernel(*refs):
        value = contract(refs[count][...], stacked(refs[:count]), weight_dim, 1)
        refs[-1][...] = value.astype(jnp.bfloat16)

    return pl.pallas_call(
        kernel,
        grid=(hidden // tile,),
        in_specs=[pl.BlockSpec((rows, depth), lambda i: (part, 0))] * count
        + [
            pl.BlockSpec((tile, depth), lambda i: (i, 0))
            if weight_dim
            else pl.BlockSpec((depth, tile), lambda i: (0, i))
        ]
        + [ANY] * len(after),
        out_specs=pl.BlockSpec((tile, count * rows), lambda i: (i, 0)),
        out_shape=jax.ShapeDtypeStruct((hidden, count * rows), jnp.bfloat16),
        compiler_params=params(16),
        name="half_terms",
    )(*blocks, weight, *after)


def gelu_call(h_terms, d_terms, w_in, after, w_held, with_dx):
    depth, hidden = w_in.shape
    cols = h_terms[0].shape[1]
    count = len(h_terms)
    row_tile = tile_of(hidden, 384)
    row_steps = hidden // row_tile
    tile = tile_of(depth, 768)
    steps = depth // tile if with_dx else 0
    part = cols // 2

    def kernel(*refs):
        h_refs, d_refs = refs[:count], refs[count : 2 * count]
        w_ref = refs[2 * count]
        outs = refs[2 * count + 1 + len(after) :]
        act_ref, d_pre_ref = outs[:2]
        step = pl.program_id(0)

        @pl.when(step < row_steps)
        def _():
            pre_act = sum(ref[...].astype(jnp.float32) for ref in h_refs)
            d_act = sum(ref[...].astype(jnp.float32) for ref in d_refs)
            value_out, slope = gelu_parts(pre_act)
            d_pre = (d_act * slope).astype(jnp.bfloat16)
            act_ref[...] = value_out.astype(jnp.bfloat16)
            d_pre_ref[...] = d_pre
            if with_dx:
                outs[-1][pl.ds(pl.multiple_of(step * row_tile, row_tile), row_tile), :] = d_pre

        if with_dx:

            @pl.when(step >= row_steps)
            def _():
                at = pl.multiple_of((step - row_steps) * tile, tile)
                left = w_ref[pl.ds(at, tile), :] if w_held else w_ref[...]
                value = contract(left, outs[-1][...], 1, 0).astype(jnp.bfloat16)
                outs[2][...] = value[:, :part]
                outs[3][...] = value[:, part:]

    low = lambda i: (jnp.minimum(i, row_steps - 1), 0)
    d_from = (d_terms[0].shape[0] - hidden) // row_tile
    high = lambda i: (jnp.minimum(i, row_steps - 1) + d_from, 0)
    h_spec, d_spec = pl.BlockSpec((row_tile, cols), low), pl.BlockSpec((row_tile, cols), high)
    shape = jax.ShapeDtypeStruct((hidden, cols), jnp.bfloat16)
    dx_spec = pl.BlockSpec((tile, part), lambda i: (jnp.maximum(i - row_steps, 0), 0))
    w_spec = pl.BlockSpec((tile, hidden), lambda i: (jnp.maximum(i - row_steps, 0), 0))
    if w_held or not with_dx:
        w_spec = HELD if with_dx else ANY
    dx_shape = jax.ShapeDtypeStruct((depth, part), jnp.bfloat16)
    return pl.pallas_call(
        kernel,
        grid=(row_steps + steps,),
        in_specs=[h_spec] * count + [d_spec] * count + [w_spec] + [ANY] * len(after),
        out_specs=[h_spec, h_spec] + [dx_spec, dx_spec] * with_dx,
        out_shape=[shape, shape] + [dx_shape, dx_shape] * with_dx,
        scratch_shapes=[pltpu.VMEM((hidden, cols), jnp.bfloat16)] * with_dx,
        compiler_params=params(12 if w_held else 20),
        name="gelu",
    )(*h_terms, *d_terms, w_in, *after)


def dx_call(d_pre, w_in, after):
    depth, hidden = w_in.shape
    cols = d_pre.shape[1]
    tile = tile_of(depth, 768)
    part = cols // 2

    def kernel(d_pre_ref, w_ref, *refs):
        value = contract(w_ref[...], d_pre_ref[...], 1, 0).astype(jnp.bfloat16)
        refs[-2][...] = value[:, :part]
        refs[-1][...] = value[:, part:]

    return pl.pallas_call(
        kernel,
        grid=(depth // tile,),
        in_specs=[
            pl.BlockSpec((hidden, cols), lambda i: (0, 0)),
            pl.BlockSpec((tile, hidden), lambda i: (i, 0)),
        ]
        + [ANY] * len(after),
        out_specs=[pl.BlockSpec((tile, part), lambda i: (i, 0))] * 2,
        out_shape=[jax.ShapeDtypeStruct((depth, part), jnp.bfloat16)] * 2,
        compiler_params=params(20),
        name="dx",
    )(d_pre, w_in, *after)


def grad_call(lefts, rights, right_at, base, after, square):
    rows, depth = lefts[0].shape
    part, cols = rights[0].shape[0] // 2, rights[0].shape[1]
    tile = tile_of(cols, 512)
    n_left, n_right = len(lefts), len(rights)
    based = base is not None

    def kernel(*refs):
        left, right = refs[:n_left], refs[n_left : n_left + n_right]
        outs = refs[n_left + n_right + int(based) + len(after) :]
        total = contract(
            jnp.concatenate([ref[...] for ref in left], axis=1) if n_left > 1 else left[0][...],
            stacked(right),
            1,
            0,
        )
        if based:
            total = total + refs[n_left + n_right][...].astype(jnp.float32)
        outs[0][...] = total.astype(jnp.bfloat16)
        if square:

            @pl.when(pl.program_id(0) == 0)
            def _():
                outs[1][...] = jnp.zeros_like(outs[1])

            outs[1][...] += jnp.sum((total * total).reshape(rows // 8, 8, tile), axis=0)

    tile_spec = pl.BlockSpec((rows, tile), lambda i: (0, i))
    out_specs = [tile_spec]
    out_shape = [jax.ShapeDtypeStruct((rows, cols), jnp.bfloat16)]
    if square:
        out_specs.append(pl.BlockSpec((8, tile), lambda i: (0, 0)))
        out_shape.append(jax.ShapeDtypeStruct((8, tile), jnp.float32))
    return pl.pallas_call(
        kernel,
        grid=(cols // tile,),
        in_specs=[pl.BlockSpec((rows, depth), lambda i: (0, 0))] * n_left
        + [pl.BlockSpec((part, tile), lambda i: (right_at, i))] * n_right
        + [tile_spec] * int(based)
        + [ANY] * len(after),
        out_specs=out_specs,
        out_shape=out_shape,
        compiler_params=params(40),
        name="grad",
    )(*lefts, *rights, *([base] if based else []), *after)


def scale_call(factor, grad, flip):
    rows, cols = grad.shape
    tile = tile_of(cols if flip else rows, 256)

    def kernel(factor_ref, in_ref, out_ref):
        value = (in_ref[...].astype(jnp.float32) * factor_ref[0, 0]).astype(jnp.bfloat16)
        out_ref[...] = value.T if flip else value

    return pl.pallas_call(
        kernel,
        grid=((cols if flip else rows) // tile,),
        in_specs=[
            pl.BlockSpec(memory_space=pltpu.SMEM),
            pl.BlockSpec((rows, tile), lambda i: (0, i))
            if flip
            else pl.BlockSpec((tile, cols), lambda i: (i, 0)),
        ],
        out_specs=pl.BlockSpec((tile, rows if flip else cols), lambda i: (i, 0)),
        out_shape=jax.ShapeDtypeStruct((cols, rows) if flip else (rows, cols), jnp.bfloat16),
        compiler_params=params(40),
        name="scale",
    )(factor.reshape(1, 1), grad)


def solution(mesh):
    n_gx, n_gy, n_gz = mesh.shape["gx"], mesh.shape["gy"], mesh.shape["gz"]

    def swap(value, mask):
        return lax.ppermute(value, "gy", [(i, i ^ mask) for i in range(n_gy)])

    def shift(value, axis, size, step):
        return lax.ppermute(value, axis, [(i, (i + step) % size) for i in range(size)])

    def over_gx(value):
        return value + sum(shift(value, "gx", n_gx, step) for step in range(1, n_gx))

    def over_gy_gz(value):
        value = value + sum(swap(value, mask) for mask in range(1, n_gy))
        return value + sum(shift(value, "gz", n_gz, step) for step in range(1, n_gz))

    def width_terms(value):
        if n_gz == 2:
            return [value, shift(value, "gz", n_gz, 1)]
        every = lax.all_gather(value, "gz")
        return [every[i] for i in range(n_gz)]

    pairs = range(0, n_gy, 2)
    leads = [(pair, step) for step in range(min(n_gx, 2)) for pair in pairs]
    leads += [(pair, step) for step in range(2, n_gx) for pair in reversed(pairs)]
    groups = [[(mask, step), (mask + 1, step)] for mask, step in leads]
    count = len(groups)
    last = count - 1
    own_tie = {last - 3: ("gin", 0), last - 2: ("gout", 0), last - 1: ("gout", 1)}
    far_tie = {last - 3: ("terms", last)}

    def shards(tokens, w_in, w_out, out_grad):
        hidden = w_in.shape[1]
        blocks = {(0, 0): jnp.concatenate([tokens, out_grad], axis=0)}
        done = ()
        terms, acts, d_pres, ties = {}, {}, {}, {}
        sums, returned = {}, []

        def later(value, *extra):
            waits = done + extra
            return lax.optimization_barrier((value, waits))[0] if waits else value

        def fetch(block, *extra):
            mask, step = block
            if mask % 2:
                blocks[block] = swap(later(blocks[mask - 1, step], *extra), 1)
            elif mask:
                blocks[block] = swap(later(blocks[0, step], *extra), mask)
            else:
                blocks[block] = shift(later(blocks[0, step - 1], *extra), "gx", n_gx, -1)

        def tie(kernel, value):
            ties.setdefault(kernel, []).append(value)

        def waits(kernel):
            return done + tuple(ties.pop(kernel, ()))

        def run_terms(g):
            nonlocal done
            blocks_of = [blocks[b] for b in groups[g]]
            value = terms_call(blocks_of, w_in_t, w_out, waits(("terms", g)), g < last)
            done = (value,)
            terms[g] = (width_terms(value),) * 2

        def plus(one, two):
            return (one.astype(jnp.float32) + two.astype(jnp.float32)).astype(jnp.bfloat16)

        def give_back(g, dx):
            pair, step = leads[g]
            sums[pair, step] = plus(dx[0], swap(dx[1], 1))
            if g < last:
                tie(own_tie.get(g, ("gelu", g + 1)), sums[pair, step])
            if pair:
                sums[pair, step] = swap(sums[pair, step], pair)
                if g < last - 1:
                    tie(far_tie.get(g, ("gelu", g + 3 - (g > 1))), sums[pair, step])
            if g < last and all((p, step) in sums for p in pairs):
                finish(step)
                if step:
                    tie(("gelu", g + 3) if g + 3 < last else ("gin", 2), returned[-1])

        def finish(step):
            total = sums[0, step]
            for p in pairs[1:]:
                total = plus(total, later(sums[p, step]) if step == n_gx - 1 else sums[p, step])
            returned.append(shift(total, "gx", n_gx, step) if step else total)

        def run_gelu(g):
            nonlocal done
            outs = gelu_call(*terms[g], w_in, waits(("gelu", g)), g < last - 2, g < last)
            acts[g], d_pres[g] = outs[:2]
            done = (outs[0],)
            if g < last:
                give_back(g, outs[2:])

        def run_grads(begin, end, name, stage, base=None):
            nonlocal done
            lefts = [(acts if name == "gout" else d_pres)[g] for g in range(begin, end)]
            rights = [blocks[b] for g in range(begin, end) for b in groups[g]]
            after = waits((name, stage))
            outs = grad_call(lefts, rights, int(name == "gout"), base, after, stage == 2)
            done = (outs[0],)
            return outs

        fetch((1, 0))
        for pair in pairs[1:]:
            fetch((pair, 0))
        fetch((0, 1))
        first = [blocks[b] for b in groups[0]]
        h_own = half_call(first, 0, w_in, 0, done)
        d_own = half_call(first, 1, w_out, 1, (h_own,))
        h_terms = width_terms(h_own)
        most = 3 * hidden // 4
        d_parts = [width_terms(d_own[:most]), width_terms(d_own[most:])]
        w_in_t = flip_call(w_in, (d_own,))
        done = (w_in_t,)
        early = (h_terms[-1], d_parts[0][-1], blocks[0, 1])
        for pair in pairs[1:]:
            fetch((pair + 1, 0), *early)
        tie(("terms", 1), blocks[0, 1])

        def next_turn(turn):
            if turn + 1 < n_gx:
                fetch((0, turn + 1))
                tie(("gelu", turn), blocks[0, turn + 1])
            if turn < n_gx:
                for pair in pairs[1:]:
                    fetch((pair, turn))
                    tie(("gelu", turn), blocks[pair, turn])
                fetch((1, turn))
            if turn > 1:
                for pair in pairs[1:]:
                    fetch((pair + 1, turn - 1))

        next_turn(1)
        for g in range(1, count):
            run_terms(g)
            if 1 < g <= n_gx:
                next_turn(g)
            if g == 1:
                others = [[later(v) for v in part[-max(1, len(part) * (n_gz > 2)) :]] for part in d_parts]
                d_terms = [jnp.concatenate(both, axis=0) for both in zip(*others)]
                terms[0] = h_terms, d_terms if n_gz > 2 else [d_own] + d_terms
            if g == last - 1:
                gin = run_grads(0, last - 2, "gin", 0)
            if g == last:
                gout = run_grads(0, last - 2, "gout", 0)
            run_gelu(g - 1)
        gin = run_grads(last - 2, last, "gin", 1, gin[0])
        gout = run_grads(last - 2, last, "gout", 1, gout[0])
        run_gelu(last)
        gin = run_grads(last, count, "gin", 2, gin[0])
        gout = run_grads(last, count, "gout", 2, gout[0])

        square = over_gx(jnp.broadcast_to(jnp.sum(gin[1]) + jnp.sum(gout[1]), (8, 128)))
        give_back(last, dx_call(d_pres[last], w_in, (square,)))
        finish(n_gx - 1)
        square = over_gy_gz(square)[0, 0]
        in_grad = sum(piece.astype(jnp.float32) for piece in returned).astype(jnp.bfloat16).T

        entries = 2.0 * (w_in.shape[0] * n_gz) * (w_in.shape[1] * n_gx * n_gy)
        factor = 1.0 / jnp.sqrt(square / entries + 1e-06)
        return in_grad, scale_call(factor, gin[0], True), scale_call(factor, gout[0], False)

    placed = (
        P(("gy", "gx"), "gz"),
        P("gz", ("gx", "gy")),
        P(("gx", "gy"), "gz"),
        P(("gy", "gx"), "gz"),
    )
    return jax.shard_map(
        shards,
        mesh=mesh,
        in_specs=placed,
        out_specs=(P(("gy", "gx"), "gz"), P("gz", ("gx", "gy")), P(("gx", "gy"), "gz")),
        check_vma=False,
    )
```

```python
import jax
import jax.numpy as jnp
from jax import lax
from jax.experimental import pallas as pl
from jax.experimental.pallas import tpu as pltpu
from jax.sharding import PartitionSpec as P

GELU_C = 0.7978845608
MIB = 1 << 20
ANY = pl.BlockSpec(memory_space=pl.ANY)
HELD = pl.BlockSpec(memory_space=pltpu.VMEM)
WIDE = 56


def gelu_parts(values):
    inner_arg = GELU_C * (values + 0.044715 * values * values * values)
    tanh_val = jnp.tanh(inner_arg)
    value_out = 0.5 * values * (1.0 + tanh_val)
    slope = 0.5 * (1.0 + tanh_val) + 0.5 * values * (1.0 - tanh_val * tanh_val) * GELU_C * (
        1.0 + 3.0 * 0.044715 * values * values
    )
    return (value_out, slope)


def contract(left, right, left_dim, right_dim):
    return lax.dot_general(
        left, right, (((left_dim,), (right_dim,)), ((), ())), preferred_element_type=jnp.float32
    )


def tile_of(extent, most):
    size = most
    while extent % size:
        size //= 2
    return size


def stacked(refs):
    return jnp.concatenate([ref[...] for ref in refs], axis=0) if len(refs) > 1 else refs[0][...]


def once(shape, at):
    return pl.BlockSpec(shape, lambda i: (at, 0), pipeline_mode=pl.Buffered(1))


def params(mib):
    return pltpu.CompilerParams(vmem_limit_bytes=mib * MIB)


def flip_call(weight, after):
    rows, cols = weight.shape
    tile = tile_of(cols, 256)

    def kernel(in_ref, *refs):
        refs[-1][...] = in_ref[...].T

    return pl.pallas_call(
        kernel,
        grid=(cols // tile,),
        in_specs=[pl.BlockSpec((rows, tile), lambda i: (0, i))] + [ANY] * len(after),
        out_specs=pl.BlockSpec((tile, rows), lambda i: (i, 0)),
        out_shape=jax.ShapeDtypeStruct((cols, rows), weight.dtype),
        compiler_params=params(6),
        name="flip",
    )(weight, *after)


def terms_call(blocks, w_in, w_out, after, split):
    hidden, depth = w_out.shape
    rows = blocks[0].shape[0] // 2
    count = len(blocks)
    tile = tile_of(hidden, 768)
    steps = hidden // tile

    def kernel(*refs):
        x_refs, dy_refs = refs[:count], refs[count : 2 * count]
        w_in_ref, w_out_ref = refs[2 * count : 2 * count + 2]
        h_ref, d_ref = (refs[-2], refs[-1]) if split else (refs[-1], refs[-1])
        step = pl.program_id(0)

        @pl.when(step < steps)
        def _():
            at = pl.ds(pl.multiple_of(step * tile, tile), tile)
            h_ref[...] = contract(w_in_ref[at, :], stacked(x_refs), 1, 1).astype(jnp.bfloat16)

        @pl.when(step >= steps)
        def _():
            at = pl.ds(pl.multiple_of((step - steps) * tile, tile), tile)
            d_ref[...] = contract(w_out_ref[at, :], stacked(dy_refs), 1, 1).astype(jnp.bfloat16)

    cols = count * rows
    out_specs = pl.BlockSpec((tile, cols), lambda i: (i, 0))
    out_shape = jax.ShapeDtypeStruct((2 * hidden, cols), jnp.bfloat16)
    if split:
        out_specs = [
            pl.BlockSpec((tile, cols), lambda i: (jnp.minimum(i, steps - 1), 0)),
            pl.BlockSpec((tile, cols), lambda i: (jnp.maximum(i - steps, 0), 0)),
        ]
        out_shape = [jax.ShapeDtypeStruct((hidden, cols), jnp.bfloat16)] * 2
    return pl.pallas_call(
        kernel,
        grid=(2 * steps,),
        in_specs=[once((rows, depth), 0)] * count
        + [once((rows, depth), 1)] * count
        + [HELD, HELD]
        + [ANY] * len(after),
        out_specs=out_specs,
        out_shape=out_shape,
        compiler_params=params(6),
        name="terms",
    )(*blocks, *blocks, w_in, w_out, *after)


def half_call(blocks, part, weight, weight_dim, after):
    depth, hidden = weight.shape[weight_dim], weight.shape[1 - weight_dim]
    rows = blocks[0].shape[0] // 2
    count = len(blocks)
    tile = tile_of(hidden, 768)

    def kernel(*refs):
        at = pl.ds(pl.multiple_of(pl.program_id(0) * tile, tile), tile)
        left = refs[count][at, :] if weight_dim else refs[count][:, at]
        refs[-1][...] = contract(left, stacked(refs[:count]), weight_dim, 1).astype(jnp.bfloat16)

    return pl.pallas_call(
        kernel,
        grid=(hidden // tile,),
        in_specs=[once((rows, depth), part)] * count
        + [HELD]
        + [ANY] * len(after),
        out_specs=pl.BlockSpec((tile, count * rows), lambda i: (i, 0)),
        out_shape=jax.ShapeDtypeStruct((hidden, count * rows), jnp.bfloat16),
        compiler_params=params(6),
        name="half_terms",
    )(*blocks, weight, *after)


def gelu_call(h_terms, d_terms, w_in, after):
    depth, hidden = w_in.shape
    cols = h_terms[0].shape[1]
    count = len(h_terms)
    row_tile = tile_of(hidden, 384)
    row_steps = hidden // row_tile
    tile = tile_of(depth, 768)
    steps = depth // tile
    part = cols // 2

    def kernel(*refs):
        h_refs, d_refs = refs[:count], refs[count : 2 * count]
        w_ref = refs[2 * count]
        outs = refs[2 * count + 1 + len(after) :]
        act_ref, d_pre_ref = outs[:2]
        held = outs[-1]
        step = pl.program_id(0)

        @pl.when(step < row_steps)
        def _():
            pre_act = sum(ref[...].astype(jnp.float32) for ref in h_refs)
            d_act = sum(ref[...].astype(jnp.float32) for ref in d_refs)
            value_out, slope = gelu_parts(pre_act)
            d_pre = (d_act * slope).astype(jnp.bfloat16)
            act_ref[...] = value_out.astype(jnp.bfloat16)
            d_pre_ref[...] = d_pre
            held[pl.ds(pl.multiple_of(step * row_tile, row_tile), row_tile), :] = d_pre

        @pl.when(step >= row_steps)
        def _():
            at = pl.ds(pl.multiple_of((step - row_steps) * tile, tile), tile)
            value = contract(w_ref[at, :], held[...], 1, 0).astype(jnp.bfloat16)
            outs[2][...] = value[:, :part]
            outs[3][...] = value[:, part:]

    low = lambda i: (jnp.minimum(i, row_steps - 1), 0)
    d_from = (d_terms[0].shape[0] - hidden) // row_tile
    high = lambda i: (jnp.minimum(i, row_steps - 1) + d_from, 0)
    h_spec, d_spec = pl.BlockSpec((row_tile, cols), low), pl.BlockSpec((row_tile, cols), high)
    shape = jax.ShapeDtypeStruct((hidden, cols), jnp.bfloat16)
    dx_spec = pl.BlockSpec((tile, part), lambda i: (jnp.maximum(i - row_steps, 0), 0))
    dx_shape = jax.ShapeDtypeStruct((depth, part), jnp.bfloat16)
    return pl.pallas_call(
        kernel,
        grid=(row_steps + steps,),
        in_specs=[h_spec] * count + [d_spec] * count + [HELD] + [ANY] * len(after),
        out_specs=[h_spec, h_spec] + [dx_spec, dx_spec],
        out_shape=[shape, shape] + [dx_shape, dx_shape],
        scratch_shapes=[pltpu.VMEM((hidden, cols), jnp.bfloat16)],
        compiler_params=params(5),
        name="gelu",
    )(*h_terms, *d_terms, w_in, *after)


def grad_call(jobs, after, square):
    rows = jobs[0][0][0].shape[0]
    part, cols = jobs[0][1][0].shape[0] // 2, jobs[0][1][0].shape[1]
    tile = tile_of(cols, 256)
    operands, specs, places = [], [], []
    tile_spec = pl.BlockSpec((rows, tile), lambda i: (0, i))
    for lefts, rights, right_at, base in jobs:
        begin = len(operands)
        operands += [*lefts, *rights, *([] if base is None else [base])]
        specs += [pl.BlockSpec((rows, lefts[0].shape[1]), lambda i: (0, 0))] * len(lefts)
        specs += [pl.BlockSpec((part, tile), lambda i, at=right_at: (at, i))] * len(rights)
        specs += [] if base is None else [tile_spec]
        middle = begin + len(lefts)
        places.append((begin, middle, middle + len(rights), base is not None))
    shape = jax.ShapeDtypeStruct((rows, cols), jnp.bfloat16)

    def kernel(*refs):
        outs = refs[len(operands) + len(after) :]
        if square:
            outs[-1][...] = jnp.zeros_like(outs[-1])

        def body(*blocks):
            for (begin, middle, end, based), out_ref in zip(places, blocks[len(operands) :]):
                left = jnp.concatenate([ref[...] for ref in blocks[begin:middle]], axis=1)
                total = contract(left, stacked(blocks[middle:end]), 1, 0)
                if based:
                    total = total + blocks[end][...].astype(jnp.float32)
                out_ref[...] = total.astype(jnp.bfloat16)
                if square:
                    outs[-1][...] += jnp.sum((total * total).reshape(rows // 8, 8, tile), axis=0)

        pltpu.emit_pipeline(
            body, grid=(cols // tile,), in_specs=specs, out_specs=[tile_spec] * len(jobs)
        )(*refs[: len(operands)], *outs[: len(jobs)])

    return pl.pallas_call(
        kernel,
        in_specs=[ANY] * (len(operands) + len(after)),
        out_specs=[ANY] * len(jobs) + [HELD] * square,
        out_shape=[shape] * len(jobs) + [jax.ShapeDtypeStruct((8, tile), jnp.float32)] * square,
        compiler_params=params(WIDE),
        name="grad",
    )(*operands, *after)


def scale_call(factor, flipped, plain, after):
    rows, cols = plain.shape
    steps = cols // tile_of(cols, 256)
    wide, high = cols // steps, rows // steps

    def kernel(factor_ref, *refs):
        def body(flipped_ref, plain_ref, grad_in_ref, grad_out_ref):
            value = flipped_ref[...].astype(jnp.float32) * factor_ref[0, 0]
            grad_in_ref[...] = value.astype(jnp.bfloat16).T
            value = plain_ref[...].astype(jnp.float32) * factor_ref[0, 0]
            grad_out_ref[...] = value.astype(jnp.bfloat16)

        high_spec = pl.BlockSpec((high, cols), lambda i: (i, 0))
        pltpu.emit_pipeline(
            body,
            grid=(steps,),
            in_specs=[pl.BlockSpec((rows, wide), lambda i: (0, i)), high_spec],
            out_specs=[pl.BlockSpec((wide, rows), lambda i: (i, 0)), high_spec],
        )(refs[0], refs[1], refs[-2], refs[-1])

    return pl.pallas_call(
        kernel,
        in_specs=[pl.BlockSpec(memory_space=pltpu.SMEM)] + [ANY] * (2 + len(after)),
        out_specs=[ANY, ANY],
        out_shape=[
            jax.ShapeDtypeStruct((cols, rows), jnp.bfloat16),
            jax.ShapeDtypeStruct((rows, cols), jnp.bfloat16),
        ],
        compiler_params=params(WIDE),
        name="scale",
    )(factor.reshape(1, 1), flipped, plain, *after)


def solution(mesh):
    n_gx, n_gy, n_gz = mesh.shape["gx"], mesh.shape["gy"], mesh.shape["gz"]

    def swap(value, mask):
        return lax.ppermute(value, "gy", [(i, i ^ mask) for i in range(n_gy)])

    def shift(value, axis, size, step):
        return lax.ppermute(value, axis, [(i, (i + step) % size) for i in range(size)])

    def over_gx(value):
        return value + sum(shift(value, "gx", n_gx, step) for step in range(1, n_gx))

    def over_gy_gz(value):
        value = value + sum(swap(value, mask) for mask in range(1, n_gy))
        return value + sum(shift(value, "gz", n_gz, step) for step in range(1, n_gz))

    def width_terms(value):
        if n_gz == 2:
            return [value, shift(value, "gz", n_gz, 1)]
        every = lax.all_gather(value, "gz")
        return [every[i] for i in range(n_gz)]

    pairs = range(0, n_gy, 2)
    leads = [(pair, step) for step in range(min(n_gx, 2)) for pair in pairs]
    leads += [(pair, step) for step in range(2, n_gx) for pair in reversed(pairs)]
    groups = [[(mask, step), (mask + 1, step)] for mask, step in leads]
    count = len(groups)
    last = count - 1
    own_tie = {last - 2: "A in", last - 1: "C", last: "norm"}
    far_tie = {last - 3: ("gelu", last - 2), last - 1: "norm"}

    def shards(tokens, w_in, w_out, out_grad):
        hidden = w_in.shape[1]
        blocks = {(0, 0): jnp.concatenate([tokens, out_grad], axis=0)}
        done = ()
        terms, acts, d_pres, ties = {}, {}, {}, {}
        sums, returned = {}, []

        def later(value, *extra):
            waits = done + extra
            return lax.optimization_barrier((value, waits))[0] if waits else value

        def fetch(block, *extra):
            mask, step = block
            if mask % 2:
                blocks[block] = swap(later(blocks[mask - 1, step], *extra), 1)
            elif mask:
                blocks[block] = swap(later(blocks[0, step], *extra), mask)
            else:
                blocks[block] = shift(later(blocks[0, step - 1], *extra), "gx", n_gx, -1)

        def tie(kernel, value):
            ties.setdefault(kernel, []).append(value)

        def waits(kernel):
            return done + tuple(ties.pop(kernel, ()))

        def run_terms(g):
            nonlocal done
            blocks_of = [blocks[b] for b in groups[g]]
            value = terms_call(blocks_of, w_in_t, w_out, waits(("terms", g)), g == last - 1)
            if g == last - 1:
                done = (value[0],)
                terms[g] = width_terms(value[0]), width_terms(value[1])
                tie(("gelu", last - 2), terms[g][0][-1])
            else:
                done = (value,)
                terms[g] = (width_terms(value),) * 2

        def plus(one, two):
            return (one.astype(jnp.float32) + two.astype(jnp.float32)).astype(jnp.bfloat16)

        def give_back(g, dx):
            pair, step = leads[g]
            sums[pair, step] = plus(dx[0], swap(dx[1], 1))
            tie(own_tie.get(g, ("gelu", g + 1)), sums[pair, step])
            if pair:
                sums[pair, step] = swap(sums[pair, step], pair)
                tie(far_tie.get(g, ("gelu", g + 3 - (g > 1))), sums[pair, step])
            if g < last and all((p, step) in sums for p in pairs):
                finish(step)
                if step:
                    tie(("gelu", min(g + 3, last - 1)), returned[-1])

        def finish(step):
            total = sums[0, step]
            for p in pairs[1:]:
                total = plus(total, later(sums[p, step]) if step == n_gx - 1 else sums[p, step])
            returned.append(shift(total, "gx", n_gx, step) if step else total)

        def run_gelu(g):
            nonlocal done
            outs = gelu_call(*terms[g], w_in, waits(("gelu", g)))
            acts[g], d_pres[g] = outs[:2]
            done = (outs[0],)
            give_back(g, outs[2:])

        def run_grads(stage, gin_from, gout_from, end, bases, square=False):
            nonlocal done
            jobs = []
            for which, begin in ((0, gin_from), (1, gout_from)):
                if begin is not None:
                    lefts = [(acts if which else d_pres)[g] for g in range(begin, end)]
                    rights = [blocks[b] for g in range(begin, end) for b in groups[g]]
                    jobs.append((lefts, rights, which, bases[which]))
            outs = grad_call(jobs, waits(stage), square)
            done = (outs[0],)
            return outs

        fetch((1, 0))
        for pair in pairs[1:]:
            fetch((pair, 0))
        fetch((0, 1))
        first = [blocks[b] for b in groups[0]]
        h_own = half_call(first, 0, w_in, 0, done)
        d_own = half_call(first, 1, w_out, 1, (h_own,))
        h_terms = width_terms(h_own)
        most = 3 * hidden // 4
        d_parts = [width_terms(d_own[:most]), width_terms(d_own[most:])]
        w_in_t = flip_call(w_in, (d_own,))
        done = (w_in_t,)
        early = (h_terms[-1], d_parts[0][-1], blocks[0, 1])
        for pair in pairs[1:]:
            fetch((pair + 1, 0), *early)
        tie(("terms", 1), blocks[0, 1])

        def next_turn(turn):
            if turn + 1 < n_gx:
                fetch((0, turn + 1))
                tie(("gelu", turn), blocks[0, turn + 1])
            if turn < n_gx:
                for pair in pairs[1:]:
                    fetch((pair, turn))
                    tie(("gelu", turn), blocks[pair, turn])
                fetch((1, turn))
            if turn > 1:
                for pair in pairs[1:]:
                    fetch((pair + 1, turn - 1))

        next_turn(1)
        none = (None, None)
        for g in range(1, count):
            run_terms(g)
            if 1 < g <= n_gx:
                next_turn(g)
            if g == 1:
                others = [[later(v) for v in part[-max(1, len(part) * (n_gz > 2)) :]] for part in d_parts]
                d_terms = [jnp.concatenate(both, axis=0) for both in zip(*others)]
                terms[0] = h_terms, d_terms if n_gz > 2 else [d_own] + d_terms
            if g < last:
                run_gelu(g - 1)
            else:
                (gin,) = run_grads("A in", 0, None, last - 1, none)
                (gout,) = run_grads("A out", None, 0, last - 1, none)
                run_gelu(g - 1)
        run_gelu(last)
        gin, gout, squares = run_grads("C", last - 1, last - 1, count, (gin, gout), True)

        finish(n_gx - 1)
        square = jnp.broadcast_to(jnp.sum(squares), (8, 128))
        square = lax.optimization_barrier((over_gx(square), waits("norm")))[0]
        square = over_gy_gz(square)[0, 0]
        in_grad = sum(piece.astype(jnp.float32) for piece in returned).astype(jnp.bfloat16).T

        entries = 2.0 * (w_in.shape[0] * n_gz) * (w_in.shape[1] * n_gx * n_gy)
        factor = 1.0 / jnp.sqrt(square / entries + 1e-06)
        return (in_grad, *scale_call(factor, gin, gout, ()))

    placed = (
        P(("gy", "gx"), "gz"),
        P("gz", ("gx", "gy")),
        P(("gx", "gy"), "gz"),
        P(("gy", "gx"), "gz"),
    )
    return jax.shard_map(
        shards,
        mesh=mesh,
        in_specs=placed,
        out_specs=(P(("gy", "gx"), "gz"), P("gz", ("gx", "gy")), P(("gx", "gy"), "gz")),
        check_vma=False,
    )
```

```python
import jax
import jax.numpy as jnp
from jax import lax
from jax.experimental import pallas as pl
from jax.experimental.pallas import tpu as pltpu
from jax.sharding import PartitionSpec as P

GELU_C = 0.7978845608
MIB = 1 << 20
WIDE = 56
ANY = pl.BlockSpec(memory_space=pl.ANY)
HELD = pl.BlockSpec(memory_space=pltpu.VMEM)


def gelu_parts(values):
    inner_arg = GELU_C * (values + 0.044715 * values * values * values)
    tanh_val = jnp.tanh(inner_arg)
    value_out = 0.5 * values * (1.0 + tanh_val)
    slope = 0.5 * (1.0 + tanh_val) + 0.5 * values * (1.0 - tanh_val * tanh_val) * GELU_C * (
        1.0 + 3.0 * 0.044715 * values * values
    )
    return (value_out, slope)


def contract(left, right, left_dim, right_dim):
    return lax.dot_general(
        left, right, (((left_dim,), (right_dim,)), ((), ())), preferred_element_type=jnp.float32
    )


def tile_of(extent, most):
    size = most
    while extent % size:
        size //= 2
    return size


def stacked(refs):
    return jnp.concatenate([ref[...] for ref in refs], axis=0) if len(refs) > 1 else refs[0][...]


def once(shape, at):
    return pl.BlockSpec(shape, lambda i: (at, 0), pipeline_mode=pl.Buffered(1))


def params(mib):
    return pltpu.CompilerParams(vmem_limit_bytes=mib * MIB)


def flip_call(weight, after):
    rows, cols = weight.shape
    tile = tile_of(cols, 256)

    def kernel(in_ref, *refs):
        refs[-1][...] = in_ref[...].T

    return pl.pallas_call(
        kernel,
        grid=(cols // tile,),
        in_specs=[pl.BlockSpec((rows, tile), lambda i: (0, i))] + [ANY] * len(after),
        out_specs=pl.BlockSpec((tile, rows), lambda i: (i, 0)),
        out_shape=jax.ShapeDtypeStruct((cols, rows), weight.dtype),
        compiler_params=params(6),
        name="flip",
    )(weight, *after)


def terms_call(blocks, w_in, w_out, after):
    hidden, depth = w_out.shape
    rows = blocks[0].shape[0] // 2
    count = len(blocks)
    tile = tile_of(hidden, 768)
    steps = hidden // tile

    def kernel(*refs):
        x_refs, dy_refs = refs[:count], refs[count : 2 * count]
        w_in_ref, w_out_ref = refs[2 * count : 2 * count + 2]
        out_ref = refs[-1]
        step = pl.program_id(0)

        @pl.when(step < steps)
        def _():
            at = pl.ds(pl.multiple_of(step * tile, tile), tile)
            out_ref[...] = contract(w_in_ref[at, :], stacked(x_refs), 1, 1).astype(jnp.bfloat16)

        @pl.when(step >= steps)
        def _():
            at = pl.ds(pl.multiple_of((step - steps) * tile, tile), tile)
            out_ref[...] = contract(w_out_ref[at, :], stacked(dy_refs), 1, 1).astype(jnp.bfloat16)

    return pl.pallas_call(
        kernel,
        grid=(2 * steps,),
        in_specs=[once((rows, depth), 0)] * count
        + [once((rows, depth), 1)] * count
        + [HELD, HELD]
        + [ANY] * len(after),
        out_specs=pl.BlockSpec((tile, count * rows), lambda i: (i, 0)),
        out_shape=jax.ShapeDtypeStruct((2 * hidden, count * rows), jnp.bfloat16),
        compiler_params=params(6),
        name="terms",
    )(*blocks, *blocks, w_in, w_out, *after)


def half_call(blocks, part, weight, weight_dim, after):
    depth, hidden = weight.shape[weight_dim], weight.shape[1 - weight_dim]
    rows = blocks[0].shape[0] // 2
    count = len(blocks)
    tile = tile_of(hidden, 768)

    def kernel(*refs):
        at = pl.ds(pl.multiple_of(pl.program_id(0) * tile, tile), tile)
        left = refs[count][at, :] if weight_dim else refs[count][:, at]
        refs[-1][...] = contract(left, stacked(refs[:count]), weight_dim, 1).astype(jnp.bfloat16)

    return pl.pallas_call(
        kernel,
        grid=(hidden // tile,),
        in_specs=[once((rows, depth), part)] * count
        + [HELD]
        + [ANY] * len(after),
        out_specs=pl.BlockSpec((tile, count * rows), lambda i: (i, 0)),
        out_shape=jax.ShapeDtypeStruct((hidden, count * rows), jnp.bfloat16),
        compiler_params=params(6),
        name="half_terms",
    )(*blocks, weight, *after)


def gelu_call(h_terms, d_terms, w_in, after):
    depth, hidden = w_in.shape
    cols = h_terms[0].shape[1]
    count = len(h_terms)
    row_tile = tile_of(hidden, 384)
    row_steps = hidden // row_tile
    tile = tile_of(depth, 768)
    steps = depth // tile
    part = cols // 2

    def kernel(*refs):
        h_refs, d_refs = refs[:count], refs[count : 2 * count]
        w_ref = refs[2 * count]
        outs = refs[2 * count + 1 + len(after) :]
        act_ref, d_pre_ref = outs[:2]
        held = outs[-1]
        step = pl.program_id(0)

        @pl.when(step < row_steps)
        def _():
            pre_act = sum(ref[...].astype(jnp.float32) for ref in h_refs)
            d_act = sum(ref[...].astype(jnp.float32) for ref in d_refs)
            value_out, slope = gelu_parts(pre_act)
            d_pre = (d_act * slope).astype(jnp.bfloat16)
            act_ref[...] = value_out.astype(jnp.bfloat16)
            d_pre_ref[...] = d_pre
            held[pl.ds(pl.multiple_of(step * row_tile, row_tile), row_tile), :] = d_pre

        @pl.when(step >= row_steps)
        def _():
            at = pl.ds(pl.multiple_of((step - row_steps) * tile, tile), tile)
            value = contract(w_ref[at, :], held[...], 1, 0).astype(jnp.bfloat16)
            outs[2][...] = value[:, :part]
            outs[3][...] = value[:, part:]

    low = lambda i: (jnp.minimum(i, row_steps - 1), 0)
    d_from = (d_terms[0].shape[0] - hidden) // row_tile
    high = lambda i: (jnp.minimum(i, row_steps - 1) + d_from, 0)
    h_spec, d_spec = pl.BlockSpec((row_tile, cols), low), pl.BlockSpec((row_tile, cols), high)
    shape = jax.ShapeDtypeStruct((hidden, cols), jnp.bfloat16)
    dx_spec = pl.BlockSpec((tile, part), lambda i: (jnp.maximum(i - row_steps, 0), 0))
    dx_shape = jax.ShapeDtypeStruct((depth, part), jnp.bfloat16)
    return pl.pallas_call(
        kernel,
        grid=(row_steps + steps,),
        in_specs=[h_spec] * count + [d_spec] * count + [HELD] + [ANY] * len(after),
        out_specs=[h_spec, h_spec] + [dx_spec, dx_spec],
        out_shape=[shape, shape] + [dx_shape, dx_shape],
        scratch_shapes=[pltpu.VMEM((hidden, cols), jnp.bfloat16)],
        compiler_params=params(5),
        name="gelu",
    )(*h_terms, *d_terms, w_in, *after)


def grad_call(jobs, after, square):
    rows = jobs[0][0][0].shape[0]
    part, cols = jobs[0][1][0].shape[0] // 2, jobs[0][1][0].shape[1]
    tile = tile_of(cols, 512)
    operands, specs, places = [], [], []
    tile_spec = pl.BlockSpec((rows, tile), lambda i: (0, i))
    out_specs, out_shape = [], []
    for lefts, rights, right_at, base in jobs:
        begin = len(operands)
        operands += [*lefts, *rights, *([] if base is None else [base])]
        specs += [once((rows, lefts[0].shape[1]), 0)] * len(lefts)
        specs += [pl.BlockSpec((part, tile), lambda i, at=right_at: (at, i))] * len(rights)
        specs += [] if base is None else [tile_spec]
        middle = begin + len(lefts)
        places.append((begin, middle, middle + len(rights), base is not None))
        out_specs.append(tile_spec)
        out_shape.append(jax.ShapeDtypeStruct((rows, cols), jnp.bfloat16))
    out_specs.append(pl.BlockSpec((8, tile), lambda i: (0, 0)))
    out_shape.append(jax.ShapeDtypeStruct((8, tile), jnp.float32))

    def kernel(*refs):
        outs = refs[len(operands) + len(after) :]

        @pl.when(pl.program_id(0) == 0)
        def _():
            outs[-1][...] = jnp.zeros_like(outs[-1])

        for (begin, middle, end, based), out_ref in zip(places, outs):
            left = jnp.concatenate([ref[...] for ref in refs[begin:middle]], axis=1)
            total = contract(left, stacked(refs[middle:end]), 1, 0)
            if based:
                total = total + refs[end][...].astype(jnp.float32)
            out_ref[...] = total.astype(jnp.bfloat16)
            if square:
                outs[-1][...] += jnp.sum((total * total).reshape(rows // 8, 8, tile), axis=0)

    return pl.pallas_call(
        kernel,
        grid=(cols // tile,),
        in_specs=specs + [ANY] * len(after),
        out_specs=out_specs,
        out_shape=out_shape,
        compiler_params=params(WIDE),
        name="grad",
    )(*operands, *after)


def scale_call(factor, grad, flip, after=()):
    rows, cols = grad.shape
    tile = tile_of(cols if flip else rows, 256)

    def kernel(factor_ref, in_ref, *refs):
        value = (in_ref[...].astype(jnp.float32) * factor_ref[0, 0]).astype(jnp.bfloat16)
        refs[-1][...] = value.T if flip else value

    return pl.pallas_call(
        kernel,
        grid=((cols if flip else rows) // tile,),
        in_specs=[
            pl.BlockSpec(memory_space=pltpu.SMEM),
            pl.BlockSpec((rows, tile), lambda i: (0, i))
            if flip
            else pl.BlockSpec((tile, cols), lambda i: (i, 0)),
        ]
        + [ANY] * len(after),
        out_specs=pl.BlockSpec((tile, rows if flip else cols), lambda i: (i, 0)),
        out_shape=jax.ShapeDtypeStruct((cols, rows) if flip else (rows, cols), jnp.bfloat16),
        compiler_params=params(40),
        name="scale",
    )(factor.reshape(1, 1), grad, *after)


def solution(mesh):
    n_gx, n_gy, n_gz = mesh.shape["gx"], mesh.shape["gy"], mesh.shape["gz"]

    def swap(value, mask):
        return lax.ppermute(value, "gy", [(i, i ^ mask) for i in range(n_gy)])

    def shift(value, axis, size, step):
        return lax.ppermute(value, axis, [(i, (i + step) % size) for i in range(size)])

    def over_gx(value):
        return value + sum(shift(value, "gx", n_gx, step) for step in range(1, n_gx))

    def over_gy_gz(value):
        value = value + sum(swap(value, mask) for mask in range(1, n_gy))
        return value + sum(shift(value, "gz", n_gz, step) for step in range(1, n_gz))

    def width_terms(value):
        if n_gz == 2:
            return [value, shift(value, "gz", n_gz, 1)]
        every = lax.all_gather(value, "gz")
        return [every[i] for i in range(n_gz)]

    pairs = range(0, n_gy, 2)
    leads = [(pair, step) for step in range(min(n_gx, 2)) for pair in pairs]
    leads += [(pair, step) for step in range(2, n_gx) for pair in reversed(pairs)]
    groups = [[(mask, step), (mask + 1, step)] for mask, step in leads]
    count = len(groups)
    last = count - 1
    own_tie = {last - 3: "A in", last - 2: "A out", last - 1: "C in", last: "C out"}
    far_tie = {last - 3: ("terms", last), last - 1: "norm"}

    def shards(tokens, w_in, w_out, out_grad):
        hidden = w_in.shape[1]
        blocks = {(0, 0): jnp.concatenate([tokens, out_grad], axis=0)}
        done = ()
        terms, acts, d_pres, ties = {}, {}, {}, {}
        sums, returned = {}, []

        def later(value, *extra):
            waits = done + extra
            return lax.optimization_barrier((value, waits))[0] if waits else value

        def fetch(block, *extra):
            mask, step = block
            if mask % 2:
                blocks[block] = swap(later(blocks[mask - 1, step], *extra), 1)
            elif mask:
                blocks[block] = swap(later(blocks[0, step], *extra), mask)
            else:
                blocks[block] = shift(later(blocks[0, step - 1], *extra), "gx", n_gx, -1)

        def tie(kernel, value):
            ties.setdefault(kernel, []).append(value)

        def waits(kernel):
            return done + tuple(ties.pop(kernel, ()))

        def run_terms(g):
            nonlocal done
            blocks_of = [blocks[b] for b in groups[g]]
            value = terms_call(blocks_of, w_in_t, w_out, waits(("terms", g)))
            done = (value,)
            terms[g] = (width_terms(value),) * 2

        def plus(one, two):
            return (one.astype(jnp.float32) + two.astype(jnp.float32)).astype(jnp.bfloat16)

        def give_back(g, dx):
            pair, step = leads[g]
            sums[pair, step] = plus(dx[0], swap(dx[1], 1))
            tie(own_tie.get(g, ("gelu", g + 1)), sums[pair, step])
            if pair:
                sums[pair, step] = swap(sums[pair, step], pair)
                tie(far_tie.get(g, ("gelu", g + 3 - (g > 1))), sums[pair, step])
            if g < last and all((p, step) in sums for p in pairs):
                finish(step)
                if step:
                    tie("C in" if g + 3 == last - 1 else ("gelu", g + 3) if g + 3 < last else "norm", returned[-1][0])

        def finish(step):
            total = sums[0, step]
            for p in pairs[1:]:
                total = plus(total, later(sums[p, step]) if step == n_gx - 1 else sums[p, step])
            half = total.shape[0] // 2 if step == n_gx - 2 else total.shape[0]
            parts = [total[at : at + half] for at in range(0, total.shape[0], half)]
            returned.append([shift(v, "gx", n_gx, step) if step else v for v in parts])

        def run_gelu(g):
            nonlocal done
            outs = gelu_call(*terms[g], w_in, waits(("gelu", g)))
            acts[g], d_pres[g] = outs[:2]
            done = (outs[0],)
            give_back(g, outs[2:])

        def run_grads(stage, gin_from, gout_from, end, bases, square=False):
            nonlocal done
            jobs = []
            for which, begin in ((0, gin_from), (1, gout_from)):
                if begin is not None:
                    lefts = [(acts if which else d_pres)[g] for g in range(begin, end)]
                    rights = [blocks[b] for g in range(begin, end) for b in groups[g]]
                    jobs.append((lefts, rights, which, bases[which]))
            outs = grad_call(jobs, waits(stage), square)
            done = (outs[-1],)
            return outs

        fetch((1, 0))
        for pair in pairs[1:]:
            fetch((pair, 0))
        fetch((0, 1))
        first = [blocks[b] for b in groups[0]]
        h_own = half_call(first, 0, w_in, 0, done)
        d_own = half_call(first, 1, w_out, 1, (h_own,))
        h_terms = width_terms(h_own)
        most = hidden // 2
        d_parts = [width_terms(d_own[:most]), width_terms(d_own[most:])]
        w_in_t = flip_call(w_in, (d_own,))
        done = (w_in_t,)
        early = (h_terms[-1], d_parts[0][-1], blocks[0, 1])
        for pair in pairs[1:]:
            fetch((pair + 1, 0), *early)
        tie(("terms", 1), blocks[0, 1])

        def next_turn(turn):
            if turn + 1 < n_gx:
                fetch((0, turn + 1))
                tie(("gelu", turn), blocks[0, turn + 1])
            if turn < n_gx:
                for pair in pairs[1:]:
                    fetch((pair, turn))
                    tie(("gelu", turn), blocks[pair, turn])
                fetch((1, turn))
            if turn > 1:
                for pair in pairs[1:]:
                    fetch((pair + 1, turn - 1))

        next_turn(1)
        none = (None, None)
        for g in range(1, count):
            run_terms(g)
            if 1 < g <= n_gx:
                next_turn(g)
            if g == 1:
                others = [[later(v) for v in part[-max(1, len(part) * (n_gz > 2)) :]] for part in d_parts]
                d_terms = [jnp.concatenate(both, axis=0) for both in zip(*others)]
                terms[0] = h_terms, d_terms if n_gz > 2 else [d_own] + d_terms
            if g == last - 1:
                gin, _ = run_grads("A in", 0, None, last - 2, none)
            run_gelu(g - 1)
        gout, _ = run_grads("A out", None, 0, last, none)
        run_gelu(last)
        gin, gin_squares = run_grads("C in", last - 2, None, count, (gin, gout), True)
        finish(n_gx - 1)
        gout, gout_squares = run_grads("C out", None, last, count, (gin, gout), True)

        square = jnp.broadcast_to(jnp.sum(gin_squares) + jnp.sum(gout_squares), (8, 128))
        square = over_gx(lax.optimization_barrier((square, waits("norm")))[0])
        square = over_gy_gz(square)[0, 0]
        pieces = [jnp.concatenate(parts, axis=0) for parts in returned]
        in_grad = sum(piece.astype(jnp.float32) for piece in pieces).astype(jnp.bfloat16).T

        entries = 2.0 * (w_in.shape[0] * n_gz) * (w_in.shape[1] * n_gx * n_gy)
        factor = 1.0 / jnp.sqrt(square / entries + 1e-06)
        grad_in = scale_call(factor, gin, True)
        return in_grad, grad_in, scale_call(factor, gout, False, (grad_in,))

    placed = (
        P(("gy", "gx"), "gz"),
        P("gz", ("gx", "gy")),
        P(("gx", "gy"), "gz"),
        P(("gy", "gx"), "gz"),
    )
    return jax.shard_map(
        shards,
        mesh=mesh,
        in_specs=placed,
        out_specs=(P(("gy", "gx"), "gz"), P("gz", ("gx", "gy")), P(("gx", "gy"), "gz")),
        check_vma=False,
    )
```

```python
import jax
import jax.numpy as jnp
from jax import lax
from jax.experimental import pallas as pl
from jax.experimental.pallas import tpu as pltpu
from jax.sharding import PartitionSpec as P

GELU_C = 0.7978845608
MIB = 1 << 20
WIDE = 56
ANY = pl.BlockSpec(memory_space=pl.ANY)
HELD = pl.BlockSpec(memory_space=pltpu.VMEM)


def gelu_parts(values):
    inner_arg = GELU_C * (values + 0.044715 * values * values * values)
    tanh_val = jnp.tanh(inner_arg)
    value_out = 0.5 * values * (1.0 + tanh_val)
    slope = 0.5 * (1.0 + tanh_val) + 0.5 * values * (1.0 - tanh_val * tanh_val) * GELU_C * (
        1.0 + 3.0 * 0.044715 * values * values
    )
    return (value_out, slope)


def contract(left, right, left_dim, right_dim):
    return lax.dot_general(
        left, right, (((left_dim,), (right_dim,)), ((), ())), preferred_element_type=jnp.float32
    )


def tile_of(extent, most):
    size = most
    while extent % size:
        size //= 2
    return size


def stacked(refs):
    return jnp.concatenate([ref[...] for ref in refs], axis=0) if len(refs) > 1 else refs[0][...]


def once(shape, at):
    return pl.BlockSpec(shape, lambda i: (at, 0), pipeline_mode=pl.Buffered(1))


def params(mib):
    return pltpu.CompilerParams(vmem_limit_bytes=mib * MIB)


def flip_call(weight, after):
    rows, cols = weight.shape
    tile = tile_of(cols, 256)

    def kernel(in_ref, *refs):
        refs[-1][...] = in_ref[...].T

    return pl.pallas_call(
        kernel,
        grid=(cols // tile,),
        in_specs=[pl.BlockSpec((rows, tile), lambda i: (0, i))] + [ANY] * len(after),
        out_specs=pl.BlockSpec((tile, rows), lambda i: (i, 0)),
        out_shape=jax.ShapeDtypeStruct((cols, rows), weight.dtype),
        compiler_params=params(6),
        name="flip",
    )(weight, *after)


def terms_call(blocks, w_in, w_out, after):
    hidden, depth = w_out.shape
    rows = blocks[0].shape[0] // 2
    count = len(blocks)
    tile = tile_of(hidden, 768)
    steps = hidden // tile

    def kernel(*refs):
        x_refs, dy_refs = refs[:count], refs[count : 2 * count]
        w_in_ref, w_out_ref = refs[2 * count : 2 * count + 2]
        out_ref = refs[-1]
        step = pl.program_id(0)

        @pl.when(step < steps)
        def _():
            at = pl.ds(pl.multiple_of(step * tile, tile), tile)
            out_ref[...] = contract(w_in_ref[at, :], stacked(x_refs), 1, 1).astype(jnp.bfloat16)

        @pl.when(step >= steps)
        def _():
            at = pl.ds(pl.multiple_of((step - steps) * tile, tile), tile)
            out_ref[...] = contract(w_out_ref[at, :], stacked(dy_refs), 1, 1).astype(jnp.bfloat16)

    return pl.pallas_call(
        kernel,
        grid=(2 * steps,),
        in_specs=[once((rows, depth), 0)] * count
        + [once((rows, depth), 1)] * count
        + [HELD, HELD]
        + [ANY] * len(after),
        out_specs=pl.BlockSpec((tile, count * rows), lambda i: (i, 0)),
        out_shape=jax.ShapeDtypeStruct((2 * hidden, count * rows), jnp.bfloat16),
        compiler_params=params(6),
        name="terms",
    )(*blocks, *blocks, w_in, w_out, *after)


def half_call(blocks, part, weight, weight_dim, after):
    depth, hidden = weight.shape[weight_dim], weight.shape[1 - weight_dim]
    rows = blocks[0].shape[0] // 2
    count = len(blocks)
    tile = tile_of(hidden, 768)

    def kernel(*refs):
        at = pl.ds(pl.multiple_of(pl.program_id(0) * tile, tile), tile)
        left = refs[count][at, :] if weight_dim else refs[count][:, at]
        refs[-1][...] = contract(left, stacked(refs[:count]), weight_dim, 1).astype(jnp.bfloat16)

    return pl.pallas_call(
        kernel,
        grid=(hidden // tile,),
        in_specs=[once((rows, depth), part)] * count
        + [HELD]
        + [ANY] * len(after),
        out_specs=pl.BlockSpec((tile, count * rows), lambda i: (i, 0)),
        out_shape=jax.ShapeDtypeStruct((hidden, count * rows), jnp.bfloat16),
        compiler_params=params(6),
        name="half_terms",
    )(*blocks, weight, *after)


def gelu_call(h_terms, d_terms, w_in, after):
    depth, hidden = w_in.shape
    cols = h_terms[0].shape[1]
    count = len(h_terms)
    row_tile = tile_of(hidden, 384)
    row_steps = hidden // row_tile
    tile = tile_of(depth, 768)
    steps = depth // tile
    part = cols // 2

    def kernel(*refs):
        h_refs, d_refs = refs[:count], refs[count : 2 * count]
        w_ref = refs[2 * count]
        outs = refs[2 * count + 1 + len(after) :]
        act_ref, d_pre_ref = outs[:2]
        held = outs[-1]
        step = pl.program_id(0)

        @pl.when(step < row_steps)
        def _():
            pre_act = sum(ref[...].astype(jnp.float32) for ref in h_refs)
            d_act = sum(ref[...].astype(jnp.float32) for ref in d_refs)
            value_out, slope = gelu_parts(pre_act)
            d_pre = (d_act * slope).astype(jnp.bfloat16)
            act_ref[...] = value_out.astype(jnp.bfloat16)
            d_pre_ref[...] = d_pre
            held[pl.ds(pl.multiple_of(step * row_tile, row_tile), row_tile), :] = d_pre

        @pl.when(step >= row_steps)
        def _():
            at = pl.ds(pl.multiple_of((step - row_steps) * tile, tile), tile)
            value = contract(w_ref[at, :], held[...], 1, 0).astype(jnp.bfloat16)
            outs[2][...] = value[:, :part]
            outs[3][...] = value[:, part:]

    low = lambda i: (jnp.minimum(i, row_steps - 1), 0)
    d_from = (d_terms[0].shape[0] - hidden) // row_tile
    high = lambda i: (jnp.minimum(i, row_steps - 1) + d_from, 0)
    h_spec, d_spec = pl.BlockSpec((row_tile, cols), low), pl.BlockSpec((row_tile, cols), high)
    shape = jax.ShapeDtypeStruct((hidden, cols), jnp.bfloat16)
    dx_spec = pl.BlockSpec((tile, part), lambda i: (jnp.maximum(i - row_steps, 0), 0))
    dx_shape = jax.ShapeDtypeStruct((depth, part), jnp.bfloat16)
    return pl.pallas_call(
        kernel,
        grid=(row_steps + steps,),
        in_specs=[h_spec] * count + [d_spec] * count + [HELD] + [ANY] * len(after),
        out_specs=[h_spec, h_spec] + [dx_spec, dx_spec],
        out_shape=[shape, shape] + [dx_shape, dx_shape],
        scratch_shapes=[pltpu.VMEM((hidden, cols), jnp.bfloat16)],
        compiler_params=params(5),
        name="gelu",
    )(*h_terms, *d_terms, w_in, *after)


def grad_call(jobs, after, square):
    rows = jobs[0][0][0].shape[0]
    part, cols = jobs[0][1][0].shape[0] // 2, jobs[0][1][0].shape[1]
    tile = tile_of(cols, 512)
    operands, specs, places = [], [], []
    tile_spec = pl.BlockSpec((rows, tile), lambda i: (0, i))
    out_specs, out_shape = [], []
    for lefts, rights, right_at, base in jobs:
        begin = len(operands)
        operands += [*lefts, *rights, *([] if base is None else [base])]
        specs += [once((rows, lefts[0].shape[1]), 0)] * len(lefts)
        specs += [pl.BlockSpec((part, tile), lambda i, at=right_at: (at, i))] * len(rights)
        specs += [] if base is None else [tile_spec]
        middle = begin + len(lefts)
        places.append((begin, middle, middle + len(rights), base is not None))
        out_specs.append(tile_spec)
        out_shape.append(jax.ShapeDtypeStruct((rows, cols), jnp.bfloat16))
    out_specs.append(pl.BlockSpec((8, tile), lambda i: (0, 0)))
    out_shape.append(jax.ShapeDtypeStruct((8, tile), jnp.float32))

    def kernel(*refs):
        outs = refs[len(operands) + len(after) :]

        @pl.when(pl.program_id(0) == 0)
        def _():
            outs[-1][...] = jnp.zeros_like(outs[-1])

        for (begin, middle, end, based), out_ref in zip(places, outs):
            left = jnp.concatenate([ref[...] for ref in refs[begin:middle]], axis=1)
            total = contract(left, stacked(refs[middle:end]), 1, 0)
            if based:
                total = total + refs[end][...].astype(jnp.float32)
            out_ref[...] = total.astype(jnp.bfloat16)
            if square:
                outs[-1][...] += jnp.sum((total * total).reshape(rows // 8, 8, tile), axis=0)

    return pl.pallas_call(
        kernel,
        grid=(cols // tile,),
        in_specs=specs + [ANY] * len(after),
        out_specs=out_specs,
        out_shape=out_shape,
        compiler_params=params(WIDE),
        name="grad",
    )(*operands, *after)


def scale_call(factor, grad, flip, after=()):
    rows, cols = grad.shape
    tile = tile_of(cols if flip else rows, 256)

    def kernel(factor_ref, in_ref, *refs):
        value = (in_ref[...].astype(jnp.float32) * factor_ref[0, 0]).astype(jnp.bfloat16)
        refs[-1][...] = value.T if flip else value

    return pl.pallas_call(
        kernel,
        grid=((cols if flip else rows) // tile,),
        in_specs=[
            pl.BlockSpec(memory_space=pltpu.SMEM),
            pl.BlockSpec((rows, tile), lambda i: (0, i))
            if flip
            else pl.BlockSpec((tile, cols), lambda i: (i, 0)),
        ]
        + [ANY] * len(after),
        out_specs=pl.BlockSpec((tile, rows if flip else cols), lambda i: (i, 0)),
        out_shape=jax.ShapeDtypeStruct((cols, rows) if flip else (rows, cols), jnp.bfloat16),
        compiler_params=params(40),
        name="scale",
    )(factor.reshape(1, 1), grad, *after)


def solution(mesh):
    n_gx, n_gy, n_gz = mesh.shape["gx"], mesh.shape["gy"], mesh.shape["gz"]

    def swap(value, mask):
        return lax.ppermute(value, "gy", [(i, i ^ mask) for i in range(n_gy)])

    def shift(value, axis, size, step):
        return lax.ppermute(value, axis, [(i, (i + step) % size) for i in range(size)])

    def over_gx(value):
        return value + sum(shift(value, "gx", n_gx, step) for step in range(1, n_gx))

    def over_gy_gz(value):
        value = value + sum(swap(value, mask) for mask in range(1, n_gy))
        return value + sum(shift(value, "gz", n_gz, step) for step in range(1, n_gz))

    def width_terms(value):
        if n_gz == 2:
            return [value, shift(value, "gz", n_gz, 1)]
        every = lax.all_gather(value, "gz")
        return [every[i] for i in range(n_gz)]

    pairs = range(0, n_gy, 2)
    leads = [(pair, step) for step in range(min(n_gx, 2)) for pair in pairs]
    leads += [(pair, step) for step in range(2, n_gx) for pair in reversed(pairs)]
    groups = [[(mask, step), (mask + 1, step)] for mask, step in leads]
    count = len(groups)
    last = count - 1
    own_tie = {last - 3: ("terms", last - 1), last - 2: "A out", last - 1: "C in", last: "C out"}
    far_tie = {last - 3: ("terms", last), last - 1: "norm"}

    def shards(tokens, w_in, w_out, out_grad):
        hidden = w_in.shape[1]
        blocks = {(0, 0): jnp.concatenate([tokens, out_grad], axis=0)}
        done = ()
        terms, acts, d_pres, ties = {}, {}, {}, {}
        sums, returned = {}, []

        def later(value, *extra):
            waits = done + extra
            return lax.optimization_barrier((value, waits))[0] if waits else value

        def fetch(block, *extra):
            mask, step = block
            if mask % 2:
                blocks[block] = swap(later(blocks[mask - 1, step], *extra), 1)
            elif mask:
                blocks[block] = swap(later(blocks[0, step], *extra), mask)
            else:
                blocks[block] = shift(later(blocks[0, step - 1], *extra), "gx", n_gx, -1)

        def tie(kernel, value):
            ties.setdefault(kernel, []).append(value)

        def waits(kernel):
            return done + tuple(ties.pop(kernel, ()))

        def run_terms(g):
            nonlocal done
            blocks_of = [blocks[b] for b in groups[g]]
            value = terms_call(blocks_of, w_in_t, w_out, waits(("terms", g)))
            done = (value,)
            terms[g] = (width_terms(value),) * 2

        def plus(one, two):
            return (one.astype(jnp.float32) + two.astype(jnp.float32)).astype(jnp.bfloat16)

        def give_back(g, dx):
            pair, step = leads[g]
            sums[pair, step] = plus(dx[0], swap(dx[1], 1))
            tie(own_tie.get(g, ("gelu", g + 1)), sums[pair, step])
            if pair:
                sums[pair, step] = swap(sums[pair, step], pair)
                tie(far_tie.get(g, ("gelu", g + 3 - (g > 1))), sums[pair, step])
            if g < last and all((p, step) in sums for p in pairs):
                finish(step)
                if step:
                    tie(("gelu", g + 3) if g + 3 < last else "norm", returned[-1][0])

        def finish(step):
            total = sums[0, step]
            for p in pairs[1:]:
                total = plus(total, later(sums[p, step]) if step == n_gx - 1 else sums[p, step])
            half = total.shape[0] // 2 if step == n_gx - 2 else total.shape[0]
            parts = [total[at : at + half] for at in range(0, total.shape[0], half)]
            returned.append([shift(v, "gx", n_gx, step) if step else v for v in parts])

        def run_gelu(g):
            nonlocal done
            outs = gelu_call(*terms[g], w_in, waits(("gelu", g)))
            acts[g], d_pres[g] = outs[:2]
            done = (outs[0],)
            give_back(g, outs[2:])

        def run_grads(stage, gin_from, gout_from, end, bases, square=False):
            nonlocal done
            jobs = []
            for which, begin in ((0, gin_from), (1, gout_from)):
                if begin is not None:
                    lefts = [(acts if which else d_pres)[g] for g in range(begin, end)]
                    rights = [blocks[b] for g in range(begin, end) for b in groups[g]]
                    jobs.append((lefts, rights, which, bases[which]))
            outs = grad_call(jobs, waits(stage), square)
            done = (outs[-1],)
            return outs

        fetch((1, 0))
        for pair in pairs[1:]:
            fetch((pair, 0))
        fetch((0, 1))
        first = [blocks[b] for b in groups[0]]
        h_own = half_call(first, 0, w_in, 0, done)
        d_own = half_call(first, 1, w_out, 1, (h_own,))
        h_terms = width_terms(h_own)
        most = hidden // 2
        d_parts = [width_terms(d_own[:most]), width_terms(d_own[most:])]
        w_in_t = flip_call(w_in, (d_own,))
        done = (w_in_t,)
        early = (h_terms[-1], d_parts[0][-1], blocks[0, 1])
        for pair in pairs[1:]:
            fetch((pair + 1, 0), *early)
        tie(("terms", 1), blocks[0, 1])

        def next_turn(turn):
            if turn + 1 < n_gx:
                fetch((0, turn + 1))
                tie(("gelu", turn), blocks[0, turn + 1])
            if turn < n_gx:
                for pair in pairs[1:]:
                    fetch((pair, turn))
                    tie(("gelu", turn), blocks[pair, turn])
                fetch((1, turn))
            if turn > 1:
                for pair in pairs[1:]:
                    fetch((pair + 1, turn - 1))

        next_turn(1)
        none = (None, None)
        for g in range(1, count):
            run_terms(g)
            if 1 < g <= n_gx:
                next_turn(g)
            if g == 1:
                others = [[later(v) for v in part[-max(1, len(part) * (n_gz > 2)) :]] for part in d_parts]
                d_terms = [jnp.concatenate(both, axis=0) for both in zip(*others)]
                terms[0] = h_terms, d_terms if n_gz > 2 else [d_own] + d_terms
            if g == last - 2:
                gin, _ = run_grads("A in", 0, None, last - 3, none)
            if g == last:
                gout, _ = run_grads("A out", None, 0, last - 1, none)
            run_gelu(g - 1)
        run_gelu(last)
        gin, gin_squares = run_grads("C in", last - 3, None, count, (gin, gout), True)
        finish(n_gx - 1)
        gout, gout_squares = run_grads("C out", None, last - 1, count, (gin, gout), True)

        square = jnp.broadcast_to(jnp.sum(gin_squares) + jnp.sum(gout_squares), (8, 128))
        square = over_gx(lax.optimization_barrier((square, waits("norm")))[0])
        square = over_gy_gz(square)[0, 0]
        pieces = [jnp.concatenate(parts, axis=0) for parts in returned]
        in_grad = sum(piece.astype(jnp.float32) for piece in pieces).astype(jnp.bfloat16).T

        entries = 2.0 * (w_in.shape[0] * n_gz) * (w_in.shape[1] * n_gx * n_gy)
        factor = 1.0 / jnp.sqrt(square / entries + 1e-06)
        grad_in = scale_call(factor, gin, True)
        return in_grad, grad_in, scale_call(factor, gout, False, (grad_in,))

    placed = (
        P(("gy", "gx"), "gz"),
        P("gz", ("gx", "gy")),
        P(("gx", "gy"), "gz"),
        P(("gy", "gx"), "gz"),
    )
    return jax.shard_map(
        shards,
        mesh=mesh,
        in_specs=placed,
        out_specs=(P(("gy", "gx"), "gz"), P("gz", ("gx", "gy")), P(("gx", "gy"), "gz")),
        check_vma=False,
    )
```
